128 devices in a mesh: row: 16 (over y, x), col: 8 (over z, core).
Axes of the slice: x: 4, y: 4, z: 4, core: 2. Of those that a mesh axis runs over, the one named last changes fastest.
Arguments:
- features: bfloat16 [131072, 128], P(('col', 'row')), may hold values from -6 to 6
- weight: bfloat16 [128, 128], replicated, may hold values from -0.5 to 0.5
- cotangent: bfloat16 [131072, 128], P(('row', 'col')), may hold values from -0.015625 to 0.015625
- tile_row: int32 [16, 8, 256], P('row', 'col'), may hold values from 0 to 31
- tile_col: int32 [16, 8, 256], P('row', 'col'), may hold values from 0 to 63
- nnz_row: int32 [16, 8, 256, 256], P('row', 'col'), may hold values from 0 to 255
- nnz_col: int32 [16, 8, 256, 256], P('row', 'col'), may hold values from 0 to 255
- edge_value: bfloat16 [16, 8, 256, 256], P('row', 'col'), may hold values from 0.019897461 to 0.19921875
- tile_count: int32 [16, 8, 256], P('row', 'col'), may hold values from 0 to 256, as said below
Outputs:
- node_out: bfloat16 [131072, 128], P(('row', 'col'))
- weight_grad: float32 [128, 128], replicated
The draws below stay inside these ranges and needn't reach their ends.
Inputs may be any that keep to these rules, and one draw needn't show every extreme that they name: `tile_count`: every device's block has a tile holding 256 live slots.
All inputs are finite; a program needn't handle non-finite values.
Results may differ from the reference program's by a relative error of at most 0.0051.
Values may be sent and summed in bfloat16 or wider, within the bound.
No kernel may reach another device: no remote copies, remote signals or barrier semaphores. Data moves between devices by JAX's collectives and lax.ppermute only.
A program may use at most 192 MiB of HBM per device.

```python
import math
import jax
import jax.numpy as jnp
from jax import lax

F = 128
TILE = 256
RB_TILES = 32
TILES_DEV = 256
NNZ_TILE = 256
NODES = 131072
CB_TILES = 64
N_ROW = 16
N_COL = 8


def draw_tile_count(key, part):
    key = jax.random.fold_in(key, 7)
    counts = jax.random.randint(key, (N_ROW, N_COL, TILES_DEV), 0, NNZ_TILE + 1)
    return counts.at[:, :, 0].set(NNZ_TILE).astype(jnp.int32)


def touch_ends(drawn, own_key, low, high):
    extent = drawn.shape
    index_at = [jax.random.randint(jax.random.fold_in(own_key, axis), (), 0, extent[axis]) for axis in range(len(extent))]
    drawn = drawn.at[tuple(index_at)].set(low)
    longest = extent.index(max(extent))
    index_at[longest] = (index_at[longest] + 1) % extent[longest]
    return drawn.at[tuple(index_at)].set(high)


def level_of(rng, extent, cuts, low, high):
    factor_of = 1.0
    for dim, blocks in cuts:
        heights = jax.random.uniform(jax.random.fold_in(jax.random.fold_in(rng, 6), dim), (blocks,), jnp.float32, low / len(cuts), high / len(cuts))
        factor_of = factor_of * jnp.repeat(jnp.exp(heights), extent[dim] // blocks).reshape((-1,) + (1,) * (len(extent) - 1 - dim))
    return factor_of


def scatter_about(rng, shape, scale, most, shards=(), kind=jnp.bfloat16):
    values = jax.random.normal(rng, shape, jnp.float32) * scale
    if len(shards) > 0:
        values = level_of(rng, shape, shards, -0.22, 0.18) * values
    return jnp.clip(values, min=-most, max=most).astype(kind)


def setup_inputs(seed: int = 0) -> dict:
    key_list = jax.random.split(jax.random.key(seed), 10)
    features = scatter_about(key_list[0], (NODES, F), 1.0, 6.0, ((0, 128),))
    weight = scatter_about(key_list[1], (F, F), F ** -0.5, 0.5)
    cotangent = scatter_about(key_list[2], (NODES, F), NODES ** -0.5, 0.015625, ((0, 128),))
    tile_row = touch_ends(jax.random.randint(key_list[3], (N_ROW, N_COL, TILES_DEV), 0, RB_TILES), jax.random.fold_in(key_list[3], 1), 0, RB_TILES - 1).astype(jnp.int32)
    tile_col = touch_ends(jax.random.randint(key_list[4], (N_ROW, N_COL, TILES_DEV), 0, CB_TILES), jax.random.fold_in(key_list[4], 1), 0, CB_TILES - 1).astype(jnp.int32)
    nnz_row = touch_ends(jax.random.randint(key_list[5], (N_ROW, N_COL, TILES_DEV, NNZ_TILE), 0, TILE), jax.random.fold_in(key_list[5], 1), 0, TILE - 1).astype(jnp.int32)
    nnz_col = touch_ends(jax.random.randint(key_list[6], (N_ROW, N_COL, TILES_DEV, NNZ_TILE), 0, TILE), jax.random.fold_in(key_list[6], 1), 0, TILE - 1).astype(jnp.int32)
    edge_value = jnp.clip(jnp.exp(math.log(0.19921875) - 2.3038113 * jax.random.uniform(key_list[7], (N_ROW, N_COL, TILES_DEV, NNZ_TILE), jnp.float32) ** level_of(key_list[7], (N_ROW, N_COL, TILES_DEV, NNZ_TILE), ((0, 16), (1, 8)), -0.2, 0.2)), 0.019897461, 0.19921875).astype(jnp.bfloat16)
    tile_count = draw_tile_count(jax.random.fold_in(key_list[9], 71), 0)
    return {"features": features, "weight": weight, "cotangent": cotangent, "tile_row": tile_row, "tile_col": tile_col, "nnz_row": nnz_row, "nnz_col": nnz_col, "edge_value": edge_value, "tile_count": tile_count}


def tile_mats(row_idx, col_idx, value_rows, count_rows):
    group, slots = row_idx.shape
    live = jnp.arange(slots, dtype=jnp.int32)[None, :] < count_rows[:, None]
    values = jnp.where(live, value_rows.astype(jnp.float32), jnp.float32(0.0))
    flat_idx = (row_idx * 256 + col_idx).astype(jnp.int32)
    flat = jnp.zeros((group, 65536), jnp.float32)
    flat = flat.at[jnp.arange(group, dtype=jnp.int32)[:, None], flat_idx].add(values)
    return flat.reshape(group, 256, 256).astype(jnp.bfloat16)


def grouped(array, group):
    return array.reshape((array.shape[0] // group, group) + array.shape[1:])


def forward_block(panel, rows, cols, nrow, ncol, values, counts, row_tiles):
    total = rows.shape[0]
    group = min(32, total)
    width = panel.shape[1]
    blocks = panel.reshape(-1, 256, width).astype(jnp.float32)
    targets = jnp.arange(row_tiles, dtype=jnp.int32)

    def step(carry, item):
        row_ids, col_ids, ridx, cidx, val, cnt = item
        tiles = tile_mats(ridx, cidx, val, cnt).astype(jnp.float32)
        picked = jnp.take(blocks, col_ids, axis=0)
        prod = jnp.einsum("gij,gjf->gif", tiles, picked, precision=lax.Precision.HIGHEST)
        onehot = (row_ids[:, None] == targets[None, :]).astype(jnp.float32)
        return carry + jnp.einsum("gk,gif->kif", onehot, prod, precision=lax.Precision.HIGHEST), None

    init = jnp.zeros((row_tiles, 256, width), jnp.float32)
    items = (grouped(rows, group), grouped(cols, group), grouped(nrow, group), grouped(ncol, group), grouped(values, group), grouped(counts, group))
    out, unused = lax.scan(step, init, items)
    return out.reshape(row_tiles * 256, width)


def backward_block(grads, rows, cols, nrow, ncol, values, counts, col_tiles):
    total = rows.shape[0]
    group = min(32, total)
    width = grads.shape[1]
    blocks = grads.reshape(-1, 256, width).astype(jnp.float32)
    targets = jnp.arange(col_tiles, dtype=jnp.int32)

    def step(carry, item):
        row_ids, col_ids, ridx, cidx, val, cnt = item
        tiles = tile_mats(ridx, cidx, val, cnt).astype(jnp.float32)
        picked = jnp.take(blocks, row_ids, axis=0)
        prod = jnp.einsum("gij,gif->gjf", tiles, picked, precision=lax.Precision.HIGHEST)
        onehot = (col_ids[:, None] == targets[None, :]).astype(jnp.float32)
        return carry + jnp.einsum("gk,gif->kif", onehot, prod, precision=lax.Precision.HIGHEST), None

    init = jnp.zeros((col_tiles, 256, width), jnp.float32)
    items = (grouped(rows, group), grouped(cols, group), grouped(nrow, group), grouped(ncol, group), grouped(values, group), grouped(counts, group))
    out, unused = lax.scan(step, init, items)
    return out.reshape(col_tiles * 256, width)


def reference(features, weight, cotangent, tile_row, tile_col, nnz_row, nnz_col, edge_value, tile_count):
    row_len = RB_TILES * 256
    col_len = CB_TILES * 256
    projected = jnp.dot(features, weight, preferred_element_type=jnp.float32).astype(jnp.bfloat16)
    devices = jnp.arange(N_ROW * N_COL, dtype=jnp.int32)

    def forward_step(pre, device):
        r = device // N_COL
        c = device % N_COL
        panel = lax.dynamic_slice_in_dim(projected, (c * col_len).astype(jnp.int32), col_len, 0)
        part = forward_block(panel, tile_row[r, c], tile_col[r, c], nnz_row[r, c], nnz_col[r, c], edge_value[r, c], tile_count[r, c], RB_TILES)
        start = (r * row_len).astype(jnp.int32)
        current = lax.dynamic_slice_in_dim(pre, start, row_len, 0)
        return lax.dynamic_update_slice_in_dim(pre, current + part, start, 0), None

    pre, unused = lax.scan(forward_step, jnp.zeros((NODES, F), jnp.float32), devices)
    node_out = jax.nn.silu(pre).astype(jnp.bfloat16)
    sig = jax.nn.sigmoid(pre)
    pre_grad = (cotangent.astype(jnp.float32) * sig * (1.0 + pre * (1.0 - sig))).astype(jnp.bfloat16)

    def backward_step(acc, device):
        r = device // N_COL
        c = device % N_COL
        rows_grad = lax.dynamic_slice_in_dim(pre_grad, (r * row_len).astype(jnp.int32), row_len, 0)
        part = backward_block(rows_grad, tile_row[r, c], tile_col[r, c], nnz_row[r, c], nnz_col[r, c], edge_value[r, c], tile_count[r, c], CB_TILES)
        start = (c * col_len).astype(jnp.int32)
        current = lax.dynamic_slice_in_dim(acc, start, col_len, 0)
        return lax.dynamic_update_slice_in_dim(acc, current + part, start, 0), None

    projected_grad, unused = lax.scan(backward_step, jnp.zeros((NODES, F), jnp.float32), devices)
    weight_grad = jnp.dot(features.astype(jnp.float32).T, projected_grad, precision=lax.Precision.HIGHEST)
    return node_out, weight_grad
```

```python
import functools

import jax
import jax.numpy as jnp
import numpy as np
from jax import lax
from jax.experimental import pallas as pl
from jax.experimental.pallas import tpu as pltpu
from jax.sharding import PartitionSpec as P

BF = jnp.bfloat16
F32 = jnp.float32
UNROLL = 8
EDGES = (0, 20, 44, 60, 64)


def row_id(y, x):
    return (y % 4) * 4 + x % 4


def col_id(z, k):
    return (z % 4) * 2 + k


def shift(a, axis, step):
    if axis == "z":
        pairs = [(col_id(z, k), col_id(z + step, k)) for z in range(4) for k in range(2)]
        return lax.ppermute(a, "col", pairs)
    dy, dx = (step, 0) if axis == "y" else (0, step)
    pairs = [(row_id(y, x), row_id(y + dy, x + dx)) for y in range(4) for x in range(4)]
    return lax.ppermute(a, "row", pairs)


def swap_cores(a):
    return lax.ppermute(a, "col", [(col_id(z, k), col_id(z, 1 - k)) for z in range(4) for k in range(2)])


def slot_table():
    table = np.zeros((4, 4, 4), np.int32)
    at = 0
    order = [
        (0, 0, range(4)), (0, 3, range(4)), (0, 1, range(4)), (3, 0, range(4)), (1, 0, range(4)),
        (0, 2, (0, 1)), (1, 3, range(4)), (0, 2, (2, 3)), (3, 1, range(4)),
        (2, 0, (0, 1)), (3, 3, range(4)), (2, 0, (2, 3)), (1, 1, range(4)),
        (2, 3, range(4)), (2, 1, range(4)), (3, 2, range(4)), (1, 2, range(4)),
        (2, 2, range(4)),
    ]
    for dy, dx, pieces in order:
        for piece in pieces:
            table[dy, dx, piece] = at
            at += 1
    return table.reshape(64)


def plan_tiles(rows, cols, counts, y, x, z, k):
    source = cols // 4
    rel = ((source // 4 - y) % 4 * 4 + (source % 4 - x) % 4) * 4 + cols % 4
    slots = jnp.sum(
        jnp.where(rel[:, None] == jnp.arange(64, dtype=jnp.int32)[None, :], slot_table()[None, :], 0), axis=1
    )
    ids = jnp.arange(256, dtype=jnp.int32)
    key = slots * 256 + ids
    rank = jnp.sum((key[None, :] < key[:, None]).astype(jnp.int32), axis=1)
    fields = jnp.stack([ids, rows, slots, counts])
    placed = jnp.sum(jnp.where(rank[None, :, None] == ids[None, None, :], fields[:, :, None], 0), axis=1)
    ends = [jnp.sum((slots < edge).astype(jnp.int32)) for edge in EDGES]
    tail = jnp.stack(ends + [z, k, z, z]).astype(jnp.int32)
    last = jnp.sum(jnp.where(jnp.arange(9)[:, None] == ids[None, :], tail[:, None], 0), axis=0)
    return jnp.concatenate([placed, last[None]], axis=0)


def spmm_kernel(phase, meta, nrow, ncol, value, pieces, *rest):
    first, final = phase == 0, phase == 3
    rest = list(rest)
    if not first:
        rest.pop(0)
    total = rest.pop(0)
    if final:
        keep, give = rest.pop(0), rest.pop(0)
    value32, iota = rest
    value32[...] = value[...].astype(F32)
    iota[...] = lax.broadcasted_iota(jnp.int32, (256, 256), 0).astype(F32).astype(BF)
    if first:
        total[...] = jnp.zeros_like(total)
    lane = lax.broadcasted_iota(jnp.int32, (1, 256), 1)
    low, high = meta[4, phase], meta[4, phase + 1]
    zero = jnp.zeros((256, 256), BF)
    one = jnp.ones((256, 256), BF)

    def step(i, carry):
        at = [low + i * UNROLL + u for u in range(UNROLL)]
        safe = [jnp.minimum(p, high - 1) for p in at]
        tiles = [meta[0, p] for p in safe]
        picked = []
        for u in range(UNROLL):
            columns = ncol[pl.ds(tiles[u], 1), :].astype(F32).astype(BF)
            gather = jnp.where(iota[...] == jnp.broadcast_to(columns, (256, 256)), one, zero)
            piece = pieces[meta[2, safe[u]] - EDGES[phase]]
            picked.append(jnp.dot(piece, gather, preferred_element_type=F32).astype(BF))
        for u in range(UNROLL):
            live = jnp.where(at[u] < high, meta[3, safe[u]], 0)
            weight = jnp.where(lane < live, value32[pl.ds(tiles[u], 1), :], 0.0).astype(BF)
            rows = nrow[pl.ds(tiles[u], 1), :].astype(F32).astype(BF)
            spread = jnp.where(
                iota[...] == jnp.broadcast_to(rows, (256, 256)), jnp.broadcast_to(weight, (256, 256)), zero
            )
            r = meta[1, safe[u]]
            total[r] = total[r] + lax.dot_general(
                picked[u], spread, (((1,), (1,)), ((), ())), preferred_element_type=F32
            )
        return carry

    lax.fori_loop(0, (high - low + UNROLL - 1) // UNROLL, step, 0)
    if final:
        z, k = meta[4, 5], meta[4, 6]
        for dz in range(4):
            zz = lax.rem(z + dz, 4) * 2
            keep[dz] = total[pl.ds((zz + k) * 4, 4)]
            give[dz] = total[pl.ds((zz + 1 - k) * 4, 4)].astype(BF)


def spmm(phase, meta, nrow, ncol, value, pieces, total=None):
    vmem = pl.BlockSpec(memory_space=pltpu.VMEM)
    args = [nrow, ncol, value, pieces] + ([] if total is None else [total])
    out = [jax.ShapeDtypeStruct((32, 128, 256), F32)]
    if phase == 3:
        out += [jax.ShapeDtypeStruct((4, 4, 128, 256), F32), jax.ShapeDtypeStruct((4, 4, 128, 256), BF)]
    share = (EDGES[phase + 1] - EDGES[phase]) / 64
    return pl.pallas_call(
        functools.partial(spmm_kernel, phase),
        out_shape=out,
        in_specs=[pl.BlockSpec(memory_space=pltpu.SMEM)] + [vmem] * len(args),
        out_specs=[vmem] * len(out),
        scratch_shapes=[pltpu.VMEM((256, 256), F32), pltpu.VMEM((256, 256), BF)],
        input_output_aliases={} if total is None else {5: 0},
        compiler_params=pltpu.CompilerParams(vmem_limit_bytes=40 << 20),
        cost_estimate=pl.CostEstimate(flops=int(share * 3.0e10), bytes_accessed=1 << 20, transcendentals=0),
        name=f"spmm_phase{phase}",
    )(meta, *args)


def finish_kernel(hidden, weight, cotangent, node_out, partial):
    h = [hidden[i] for i in range(4)]
    w = weight[...].astype(F32)
    grad = jnp.zeros((128, 128), F32)
    for i in range(4):
        pre_t = lax.dot_general(
            w, h[i], (((0,), (0,)), ((), ())), precision=lax.Precision.HIGHEST, preferred_element_type=F32
        )
        pre = pre_t.T
        sig = 1.0 / (1.0 + jnp.exp(-pre))
        span = pl.ds(i * 256, 256)
        node_out[span, :] = (pre * sig).astype(BF)
        slope = sig * (1.0 + pre * (1.0 - sig))
        pre_grad = (cotangent[span, :].astype(F32) * slope).astype(BF).astype(F32)
        grad = grad + jnp.dot(h[i], pre_grad, precision=lax.Precision.HIGHEST, preferred_element_type=F32)
    partial[...] = grad


def finish(hidden, weight, cotangent):
    vmem = pl.BlockSpec(memory_space=pltpu.VMEM)
    return pl.pallas_call(
        finish_kernel,
        out_shape=[jax.ShapeDtypeStruct((1024, 128), BF), jax.ShapeDtypeStruct((128, 128), F32)],
        in_specs=[vmem] * 3,
        out_specs=[vmem] * 2,
        compiler_params=pltpu.CompilerParams(vmem_limit_bytes=16 << 20),
        name="finish",
    )(hidden, weight, cotangent)


def cat(*parts):
    return jnp.concatenate(parts, axis=0)


def add(a, b):
    return a.astype(F32) + b.astype(F32)


def sum_ring(v, axis):
    return (v + shift(v, axis, 2)) + (shift(v, axis, 1) + shift(v, axis, -1))


def body(features, weight, cotangent, tile_row, tile_col, nnz_row, nnz_col, edge_value, tile_count):
    row, col = lax.axis_index("row"), lax.axis_index("col")
    meta = plan_tiles(
        tile_row.reshape(256), tile_col.reshape(256), tile_count.reshape(256),
        row // 4, row % 4, col // 2, col % 2,
    )
    slots = (meta, nnz_row.reshape(256, 256), nnz_col.reshape(256, 256), edge_value.reshape(256, 256))

    own = jnp.transpose(features.reshape(4, 256, 128), (0, 2, 1))
    r1, l1 = shift(own, "x", 1), shift(own, "x", -1)
    d1, u1 = shift(own, "y", 1), shift(own, "y", -1)
    r2, l2 = shift(cat(r1[:2], u1), "x", 1), shift(cat(l1[2:], d1), "x", -1)
    d2, u2 = shift(cat(d1[:2], r1), "y", 1), shift(cat(u1[2:], l1), "y", -1)
    (total,) = spmm(0, *slots, cat(own, r1, l1, d1, u1))
    across, along = cat(r2[:2], l2[:2]), cat(d2[:2], u2[:2])
    r3, l3 = shift(along, "x", 1), shift(along, "x", -1)
    d3, u3 = shift(across, "y", 1), shift(across, "y", -1)
    (total,) = spmm(1, *slots, cat(r2, l2, d2, u2), total)
    r4, l4 = shift(r3[0:1], "x", 1), shift(l3[1:2], "x", -1)
    d4, u4 = shift(d3[2:3], "y", 1), shift(u3[3:4], "y", -1)
    (total,) = spmm(2, *slots, cat(r3, l3, d3, u3), total)
    total, keep, give = spmm(3, *slots, cat(r4, l4, d4, u4), total)

    got = swap_cores(give)
    mine = add(keep[0], got[0])
    far = add(keep[2], got[2]).astype(BF)
    up32, down32 = add(keep[1], got[1]), add(keep[3], got[3])
    far_up = shift(far[:2], "z", 1)
    far_down = shift(far[2:], "z", -1)
    near_up = shift(up32[2:].astype(BF), "z", 1)
    near_down = shift(down32[:2].astype(BF), "z", -1)
    sum_up = shift(add(up32[:2], far_up).astype(BF), "z", 1)
    sum_down = shift(add(down32[2:], far_down).astype(BF), "z", -1)
    hidden = mine + cat(add(sum_up, near_down), add(near_up, sum_down))

    node_out, partial = finish(hidden, weight, cotangent)
    grad = partial + swap_cores(partial)
    for axis in ("z", "x", "y"):
        grad = sum_ring(grad, axis)
    return node_out, grad


def solution(mesh):
    placed = (
        P(("col", "row"), None),
        P(),
        P(("row", "col"), None),
        P("row", "col", None),
        P("row", "col", None),
        P("row", "col", None, None),
        P("row", "col", None, None),
        P("row", "col", None, None),
        P("row", "col", None),
    )
    return jax.shard_map(
        body, mesh=mesh, in_specs=placed, out_specs=(P(("row", "col"), None), P()), check_vma=False
    )
```

```python
import functools

import jax
import jax.numpy as jnp
import numpy as np
from jax import lax
from jax.experimental import pallas as pl
from jax.experimental.pallas import tpu as pltpu
from jax.sharding import PartitionSpec as P

BF = jnp.bfloat16
F32 = jnp.float32
UNROLL = 8
FIRST = (0, 20, 44, 44)
WIDTH = (20, 24, 20, 20)


def row_id(y, x):
    return (y % 4) * 4 + x % 4


def col_id(z, k):
    return (z % 4) * 2 + k


def shift(a, axis, step):
    if axis == "z":
        pairs = [(col_id(z, k), col_id(z + step, k)) for z in range(4) for k in range(2)]
        return lax.ppermute(a, "col", pairs)
    dy, dx = {"y": (step, 0), "x": (0, step), "yx": (step, step)}[axis]
    pairs = [(row_id(y, x), row_id(y + dy, x + dx)) for y in range(4) for x in range(4)]
    return lax.ppermute(a, "row", pairs)


def swap_cores(a):
    return lax.ppermute(a, "col", [(col_id(z, k), col_id(z, 1 - k)) for z in range(4) for k in range(2)])


def slot_table():
    table = np.zeros((4, 4, 4), np.int32)
    at = 0
    order = [
        (0, 0, range(4)), (0, 3, range(4)), (0, 1, range(4)), (3, 0, range(4)), (1, 0, range(4)),
        (0, 2, (0, 1)), (1, 3, range(4)), (0, 2, (2, 3)), (3, 1, range(4)),
        (2, 0, (0, 1)), (3, 3, range(4)), (2, 0, (2, 3)), (1, 1, range(4)),
        (2, 3, range(4)), (2, 1, range(4)), (3, 2, range(4)), (1, 2, range(4)),
        (2, 2, range(4)),
    ]
    for dy, dx, pieces in order:
        for piece in pieces:
            table[dy, dx, piece] = at
            at += 1
    return table.reshape(64)


def plan_tiles(rows, cols, counts, y, x, z, k):
    source = cols // 4
    rel = ((source // 4 - y) % 4 * 4 + (source % 4 - x) % 4) * 4 + cols % 4
    slots = jnp.sum(
        jnp.where(rel[:, None] == jnp.arange(64, dtype=jnp.int32)[None, :], slot_table()[None, :], 0), axis=1
    )
    ids = jnp.arange(256, dtype=jnp.int32)
    near = (rows // 8 != (z + 2) % 4).astype(jnp.int32)
    phase = jnp.where(slots < FIRST[1], 0, jnp.where(slots < FIRST[2], 1, 2 + near))
    key = phase * 256 + ids
    rank = jnp.sum((key[None, :] < key[:, None]).astype(jnp.int32), axis=1)
    fields = jnp.stack([ids, rows, slots, counts])
    placed = jnp.sum(jnp.where(rank[None, :, None] == ids[None, None, :], fields[:, :, None], 0), axis=1)
    starts = jnp.sum((phase[None, :] < ids[:, None]).astype(jnp.int32), axis=1)
    last = jnp.where(ids < 5, starts, jnp.where(ids == 5, z, k))
    return jnp.concatenate([placed, last[None]], axis=0)


def spmm_kernel(phase, meta, nrow, ncol, value, pieces, *rest):
    first = phase == 0
    rest = list(rest)
    if not first:
        rest.pop(0)
    total = rest.pop(0)
    if phase >= 2:
        keep, give = rest.pop(0), rest.pop(0)
    value32, iota = rest
    value32[...] = value[...].astype(F32)
    iota[...] = lax.broadcasted_iota(jnp.int32, (256, 256), 0).astype(F32).astype(BF)
    if first:
        total[...] = jnp.zeros_like(total)
    lane = lax.broadcasted_iota(jnp.int32, (1, 256), 1)
    low, high = meta[4, phase], meta[4, phase + 1]
    zero = jnp.zeros((256, 256), BF)
    one = jnp.ones((256, 256), BF)

    def step(i, carry):
        at = [low + i * UNROLL + u for u in range(UNROLL)]
        safe = [jnp.minimum(p, high - 1) for p in at]
        tiles = [meta[0, p] for p in safe]
        picked = []
        for u in range(UNROLL):
            columns = ncol[pl.ds(tiles[u], 1), :].astype(F32).astype(BF)
            gather = jnp.where(iota[...] == jnp.broadcast_to(columns, (256, 256)), one, zero)
            piece = pieces[meta[2, safe[u]] - FIRST[phase]]
            picked.append(jnp.dot(piece, gather, preferred_element_type=F32).astype(BF))
        for u in range(UNROLL):
            live = jnp.where(at[u] < high, meta[3, safe[u]], 0)
            weight = jnp.where(lane < live, value32[pl.ds(tiles[u], 1), :], 0.0).astype(BF)
            rows = nrow[pl.ds(tiles[u], 1), :].astype(F32).astype(BF)
            spread = jnp.where(
                iota[...] == jnp.broadcast_to(rows, (256, 256)), jnp.broadcast_to(weight, (256, 256)), zero
            )
            r = meta[1, safe[u]]
            total[r] = total[r] + lax.dot_general(
                picked[u], spread, (((1,), (1,)), ((), ())), preferred_element_type=F32
            )
        return carry

    lax.fori_loop(0, (high - low + UNROLL - 1) // UNROLL, step, 0)
    if phase >= 2:
        z, k = meta[4, 5], meta[4, 6]
        for i, dz in enumerate(((2,), (0, 1, 3))[phase - 2]):
            zz = lax.rem(z + dz, 4) * 2
            keep[i] = total[pl.ds((zz + k) * 4, 4)]
            give[i] = total[pl.ds((zz + 1 - k) * 4, 4)].astype(BF)


def spmm(phase, meta, nrow, ncol, value, pieces, total=None):
    vmem = pl.BlockSpec(memory_space=pltpu.VMEM)
    args = [nrow, ncol, value, pieces] + ([] if total is None else [total])
    out = [jax.ShapeDtypeStruct((32, 128, 256), F32)]
    if phase >= 2:
        blocks = (1, 3)[phase - 2]
        out += [jax.ShapeDtypeStruct((blocks, 4, 128, 256), F32), jax.ShapeDtypeStruct((blocks, 4, 128, 256), BF)]
    share = WIDTH[phase] / 64 * (1.0, 1.0, 0.25, 0.75)[phase]
    return pl.pallas_call(
        functools.partial(spmm_kernel, phase),
        out_shape=out,
        in_specs=[pl.BlockSpec(memory_space=pltpu.SMEM)] + [vmem] * len(args),
        out_specs=[vmem] * len(out),
        scratch_shapes=[pltpu.VMEM((256, 256), F32), pltpu.VMEM((256, 256), BF)],
        input_output_aliases={} if total is None else {5: 0},
        compiler_params=pltpu.CompilerParams(vmem_limit_bytes=40 << 20),
        cost_estimate=pl.CostEstimate(flops=int(share * 3.0e10), bytes_accessed=1 << 20, transcendentals=0),
        name=f"spmm_phase{phase}",
    )(meta, *args)


def finish_kernel(col, hidden, weight, cotangent, node_out, keep, give):
    h = [hidden[i] for i in range(4)]
    w = weight[...].astype(F32)
    grad = jnp.zeros((128, 128), F32)
    for i in range(4):
        pre_t = lax.dot_general(
            w, h[i], (((0,), (0,)), ((), ())), precision=lax.Precision.HIGHEST, preferred_element_type=F32
        )
        pre = pre_t.T
        sig = 1.0 / (1.0 + jnp.exp(-pre))
        span = pl.ds(i * 256, 256)
        node_out[span, :] = (pre * sig).astype(BF)
        slope = sig * (1.0 + pre * (1.0 - sig))
        pre_grad = (cotangent[span, :].astype(F32) * slope).astype(BF).astype(F32)
        grad = grad + jnp.dot(h[i], pre_grad, precision=lax.Precision.HIGHEST, preferred_element_type=F32)
    low = lax.rem(col[0], 2) == 0
    keep[...] = jnp.where(low, grad[:64], grad[64:])
    give[...] = jnp.where(low, grad[64:], grad[:64])


def finish(col, hidden, weight, cotangent):
    vmem = pl.BlockSpec(memory_space=pltpu.VMEM)
    return pl.pallas_call(
        finish_kernel,
        out_shape=[jax.ShapeDtypeStruct((1024, 128), BF)] + [jax.ShapeDtypeStruct((64, 128), F32)] * 2,
        in_specs=[pl.BlockSpec(memory_space=pltpu.SMEM)] + [vmem] * 3,
        out_specs=[vmem] * 3,
        compiler_params=pltpu.CompilerParams(vmem_limit_bytes=16 << 20),
        name="finish",
    )(col.reshape(1), hidden, weight, cotangent)


def cat(*parts):
    return jnp.concatenate(parts, axis=0)


def add(a, b):
    return a.astype(F32) + b.astype(F32)


def sum_ring(v, axis):
    return (v + shift(v, axis, 2)) + (shift(v, axis, 1) + shift(v, axis, -1))


def body(features, weight, cotangent, tile_row, tile_col, nnz_row, nnz_col, edge_value, tile_count):
    row, col = lax.axis_index("row"), lax.axis_index("col")
    meta = plan_tiles(
        tile_row.reshape(256), tile_col.reshape(256), tile_count.reshape(256),
        row // 4, row % 4, col // 2, col % 2,
    )
    slots = (meta, nnz_row.reshape(256, 256), nnz_col.reshape(256, 256), edge_value.reshape(256, 256))

    own = jnp.transpose(features.reshape(4, 256, 128), (0, 2, 1))
    r1, l1 = shift(own, "x", 1), shift(own, "x", -1)
    d1, u1 = shift(own, "y", 1), shift(own, "y", -1)
    r2, l2 = shift(cat(r1[:2], u1), "x", 1), shift(cat(l1[2:], d1), "x", -1)
    d2, u2 = shift(cat(d1[:2], r1), "y", 1), shift(cat(u1[2:], l1), "y", -1)
    (total,) = spmm(0, *slots, cat(own, r1, l1, d1, u1))
    across, along = cat(r2[:2], l2[:2]), cat(d2[:2], u2[:2])
    r3, l3 = shift(along, "x", 1), shift(along, "x", -1)
    d3, u3 = shift(across, "y", 1), shift(across, "y", -1)
    (total,) = spmm(1, *slots, cat(r2, l2, d2, u2), total)
    a3, b3 = shift(d2[2:4], "yx", 1), shift(u2[4:6], "yx", -1)
    last = cat(r3, l3, d3, u3, a3, b3)

    total, keep, give = spmm(2, *slots, last, total)
    far = add(keep[0], swap_cores(give)[0]).astype(BF)
    far_up, far_down = shift(far[:2], "z", 1), shift(far[2:], "z", -1)
    total, keep, give = spmm(3, *slots, last, total)
    got = swap_cores(give)
    mine, up, down = add(keep[0], got[0]), add(keep[1], got[1]), add(keep[2], got[2])
    up = shift(cat(add(up[:2], far_up), up[2:]).astype(BF), "z", 1)
    down = shift(cat(down[:2], add(down[2:], far_down)).astype(BF), "z", -1)
    hidden = mine + add(up, down)

    node_out, grad, other = finish(col, hidden, weight, cotangent)
    grad = grad + swap_cores(other)
    for axis in ("z", "x", "y"):
        grad = sum_ring(grad, axis)
    other = swap_cores(grad)
    grad = jnp.where(col % 2 == 0, cat(grad, other), cat(other, grad))
    return node_out, grad


def solution(mesh):
    placed = (
        P(("col", "row"), None),
        P(),
        P(("row", "col"), None),
        P("row", "col", None),
        P("row", "col", None),
        P("row", "col", None, None),
        P("row", "col", None, None),
        P("row", "col", None, None),
        P("row", "col", None),
    )
    return jax.shard_map(
        body, mesh=mesh, in_specs=placed, out_specs=(P(("row", "col"), None), P()), check_vma=False
    )
```

```python
import functools

import jax
import jax.numpy as jnp
from jax import lax
from jax.experimental import pallas as pl
from jax.experimental.pallas import tpu as pltpu
from jax.sharding import PartitionSpec as P

BF = jnp.bfloat16
F32 = jnp.float32
UNROLL = 16
FIRST = (0, 16, 40, 40)
PLUS = 6


def permute(a, move):
    pairs = []
    for i in range(128):
        y, x, z, k = i // 32, i // 8 % 4, i // 2 % 4, i % 2
        y, x, z, k = (v % 4 for v in move(y, x, z, k))
        pairs.append((i, y * 32 + x * 8 + z * 2 + k))
    return lax.ppermute(a, ("row", "col"), pairs)


def first_axis(a, step):
    return permute(a, lambda y, x, z, k: (y + step * k, x + step * (1 - k), z, k))


def second_axis(a, step):
    return permute(a, lambda y, x, z, k: (y + step * (1 - k), x + step * k, z, k))


def swap_cores(a):
    return permute(a, lambda y, x, z, k: (y, x, z, 1 - k))


def shift(a, axis, step):
    by = [step * (axis == name) for name in "yxz"]
    return permute(a, lambda y, x, z, k: (y + by[0], x + by[1], z + by[2], k))


def plan_tiles(rows, cols, counts, y, x, z, k):
    source = cols // 4
    dy, dx = (source // 4 - y) % 4, (source % 4 - x) % 4
    near, far = jnp.where(k == 0, dx, dy), jnp.where(k == 0, dy, dx)
    triple = (near - (near == 3)) * 4
    slots = cols % 4 + jnp.where(
        far == 0,
        near * 4,
        jnp.where(
            near == 2,
            jnp.where(far == 3, 40, jnp.where(far == 1, 44, 60)),
            triple + jnp.where(far == 1, 16, jnp.where(far == 3, 28, 48)),
        ),
    )
    ids = jnp.arange(256, dtype=jnp.int32)
    owner, ahead = rows // 4 % 2, (rows // 8) ^ z
    away = (ahead == 2) | (ahead == 1 + 2 * owner)
    phase = jnp.where(slots < 16, 0, jnp.where(slots < 40, 1, jnp.where(away, 2, 3)))
    group = phase * 2 + (counts <= 128).astype(jnp.int32)
    key = group * 256 + ids
    rank = jnp.sum((key[None, :] < key[:, None]).astype(jnp.int32), axis=1)
    fields = jnp.stack([ids, rows, slots, counts])
    placed = jnp.sum(jnp.where(rank[None, :, None] == ids[None, None, :], fields[:, :, None], 0), axis=1)
    starts = jnp.sum((group[None, :] < ids[:, None]).astype(jnp.int32), axis=1)
    last = jnp.where(ids < 9, starts, jnp.where(ids == 9, z, k))
    return jnp.concatenate([placed, last[None]], axis=0)


def spmm_kernel(phase, meta, nrow, ncol, value, pieces, *rest):
    rest = list(rest)
    if phase > 0:
        rest.pop(0)
    total = rest.pop(0)
    if phase >= 2:
        keep, give = rest.pop(0), rest.pop(0)
    value32, iota = rest
    value32[...] = value[...].astype(F32)
    iota[...] = lax.broadcasted_iota(jnp.int32, (256, 256), 0).astype(F32).astype(BF)
    if phase == 0:
        total[...] = jnp.zeros_like(total)
    low, middle, high = meta[4, 2 * phase], meta[4, 2 * phase + 1], meta[4, 2 * phase + 2]

    def run(width, begin, steps):
        lane = lax.broadcasted_iota(jnp.int32, (1, width), 1)
        zero = jnp.zeros((256, width), BF)
        one = jnp.ones((256, width), BF)

        def line(ref, tile):
            return ref[pl.ds(tile, 1), :][:, :width]

        def spread(picture, hot):
            index = jnp.broadcast_to(picture.astype(F32).astype(BF), (256, width))
            return jnp.where(iota[:, :width] == index, hot, zero)

        def step(i, carry):
            at = [begin + i * UNROLL + u for u in range(UNROLL)]
            safe = [jnp.minimum(p, high - 1) for p in at]
            tiles = [meta[0, p] for p in safe]
            picked = []
            for u in range(UNROLL):
                piece = pieces[meta[2, safe[u]] - FIRST[phase]]
                columns = spread(line(ncol, tiles[u]), one)
                picked.append(jnp.dot(piece, columns, preferred_element_type=F32).astype(BF))
            for u in range(UNROLL):
                live = jnp.where(at[u] < high, meta[3, safe[u]], 0)
                weight = jnp.where(lane < live, line(value32, tiles[u]), 0.0).astype(BF)
                rows = spread(line(nrow, tiles[u]), jnp.broadcast_to(weight, (256, width)))
                r = meta[1, safe[u]]
                total[r] = total[r] + lax.dot_general(
                    rows, picked[u], (((1,), (1,)), ((), ())), preferred_element_type=F32
                )
            return carry

        lax.fori_loop(0, steps, step, 0)

    wide = (middle - low + UNROLL - 1) // UNROLL
    run(256, low, wide)
    begin = jnp.minimum(low + wide * UNROLL, high)
    run(128, begin, (high - begin + UNROLL - 1) // UNROLL)
    if phase >= 2:
        z, k = meta[4, 9], meta[4, 10]
        near, other = 1 + 2 * k, 3 - 2 * k
        ahead = ((near, other), (2, 2)) if phase == 2 else ((0, 0), (other, near))
        for i, (e_keep, e_give) in enumerate(ahead):
            keep[i] = total[pl.ds(((z ^ e_keep) * 2 + k) * 4, 4)]
            give[i] = total[pl.ds(((z ^ e_give) * 2 + 1 - k) * 4, 4)].astype(BF)


def spmm(phase, meta, nrow, ncol, value, pieces, total=None):
    vmem = pl.BlockSpec(memory_space=pltpu.VMEM)
    args = [nrow, ncol, value, pieces] + ([] if total is None else [total])
    out = [jax.ShapeDtypeStruct((32, 256, 128), F32)]
    if phase >= 2:
        out += [jax.ShapeDtypeStruct((2, 4, 256, 128), F32), jax.ShapeDtypeStruct((2, 4, 256, 128), BF)]
    share = (16, 24, 12, 12)[phase] / 64
    return pl.pallas_call(
        functools.partial(spmm_kernel, phase),
        out_shape=out,
        in_specs=[pl.BlockSpec(memory_space=pltpu.SMEM)] + [vmem] * len(args),
        out_specs=[vmem] * len(out),
        scratch_shapes=[pltpu.VMEM((256, 256), F32), pltpu.VMEM((256, 256), BF)],
        input_output_aliases={} if total is None else {5: 0},
        compiler_params=pltpu.CompilerParams(vmem_limit_bytes=40 << 20),
        cost_estimate=pl.CostEstimate(flops=int(share * 2.0e10), bytes_accessed=1 << 20, transcendentals=0),
        name=f"spmm_phase{phase}",
    )(meta, *args)


def finish_kernel(col, hidden, weight, cotangent, node_out, keep, give):
    w = weight[...].astype(F32)
    grad = jnp.zeros((128, 128), F32)
    for i in range(4):
        h = hidden[i]
        pre = jnp.dot(h, w, precision=lax.Precision.HIGHEST, preferred_element_type=F32)
        sig = 1.0 / (1.0 + jnp.exp(-pre))
        span = pl.ds(i * 256, 256)
        node_out[span, :] = (pre * sig).astype(BF)
        slope = sig * (1.0 + pre * (1.0 - sig))
        pre_grad = (cotangent[span, :].astype(F32) * slope).astype(BF).astype(F32)
        grad = grad + lax.dot_general(
            h, pre_grad, (((0,), (0,)), ((), ())), precision=lax.Precision.HIGHEST, preferred_element_type=F32
        )
    low = lax.rem(col[0], 2) == 0
    keep[...] = jnp.where(low, grad[:64], grad[64:])
    give[...] = jnp.where(low, grad[64:], grad[:64])


def finish(col, hidden, weight, cotangent):
    vmem = pl.BlockSpec(memory_space=pltpu.VMEM)
    return pl.pallas_call(
        finish_kernel,
        out_shape=[jax.ShapeDtypeStruct((1024, 128), BF)] + [jax.ShapeDtypeStruct((64, 128), F32)] * 2,
        in_specs=[pl.BlockSpec(memory_space=pltpu.SMEM)] + [vmem] * 3,
        out_specs=[vmem] * 3,
        compiler_params=pltpu.CompilerParams(vmem_limit_bytes=16 << 20),
        name="finish",
    )(col.reshape(1), hidden, weight, cotangent)


def transpose_kernel(features, out):
    for i in range(4):
        out[i] = features[pl.ds(i * 256, 256), :].T


def transposed(features):
    vmem = pl.BlockSpec(memory_space=pltpu.VMEM)
    return pl.pallas_call(
        transpose_kernel,
        out_shape=jax.ShapeDtypeStruct((4, 128, 256), BF),
        in_specs=[vmem],
        out_specs=vmem,
        compiler_params=pltpu.CompilerParams(vmem_limit_bytes=8 << 20),
        name="transposed",
    )(features)


def cat(*parts):
    return jnp.concatenate(parts, axis=0)


def add(a, b):
    return a.astype(F32) + b.astype(F32)


def sum_ring(v, axis):
    return (v + shift(v, axis, 2)) + (shift(v, axis, 1) + shift(v, axis, -1))


def body(features, weight, cotangent, tile_row, tile_col, nnz_row, nnz_col, edge_value, tile_count):
    row, col = lax.axis_index("row"), lax.axis_index("col")
    meta = plan_tiles(
        tile_row.reshape(256), tile_col.reshape(256), tile_count.reshape(256),
        row // 4, row % 4, col // 2, col % 2,
    )
    slots = (meta, nnz_row.reshape(256, 256), nnz_col.reshape(256, 256), edge_value.reshape(256, 256))

    own = transposed(features)
    right, left = first_axis(own, 1), first_axis(own, -1)
    opposite = first_axis(own, 2)
    near = cat(own, left, right)
    down, up = second_axis(near, 1), second_axis(near, -1)
    corner = second_axis(opposite, 2)
    (total,) = spmm(0, *slots, cat(own, left, opposite, right))
    plus = second_axis(cat(opposite, down[:PLUS]), 1)
    minus = second_axis(cat(opposite, up[PLUS:]), -1)
    (total,) = spmm(1, *slots, cat(up, down), total)
    rest = cat(plus[:4], minus[:4], plus[4:], minus[4:], corner)
    total, keep, give = spmm(2, *slots, rest, total)

    away = add(keep, swap_cores(give)).astype(BF)
    away, total = lax.optimization_barrier((away, total))
    got = permute(away, lambda y, x, z, k: (y, x, z ^ (1 + 2 * k), k))
    total, keep, give = spmm(3, *slots, rest, total)
    give, got = lax.optimization_barrier((give, got))
    home = add(keep, swap_cores(give))
    mine, pair = add(home[0], got[0]), add(home[1], got[1])
    hidden = add(mine, permute(pair.astype(BF), lambda y, x, z, k: (y, x, z ^ (3 - 2 * k), k)))

    node_out, grad, other = finish(col, hidden, weight, cotangent)
    grad = grad + swap_cores(other)
    for axis in ("z", "x", "y"):
        grad = sum_ring(grad, axis)
    other = swap_cores(grad)
    grad = jnp.where(col % 2 == 0, cat(grad, other), cat(other, grad))
    return node_out, grad


def solution(mesh):
    placed = (
        P(("col", "row"), None),
        P(),
        P(("row", "col"), None),
        P("row", "col", None),
        P("row", "col", None),
        P("row", "col", None, None),
        P("row", "col", None, None),
        P("row", "col", None, None),
        P("row", "col", None),
    )
    return jax.shard_map(
        body, mesh=mesh, in_specs=placed, out_specs=(P(("row", "col"), None), P()), check_vma=False
    )
```

```python
import functools

import jax
import jax.numpy as jnp
from jax import lax
from jax.experimental import pallas as pl
from jax.experimental.pallas import tpu as pltpu
from jax.sharding import PartitionSpec as P

BF = jnp.bfloat16
F32 = jnp.float32
UNROLL = 16
FIRST = (0, 16, 40, 40)
PLUS = 6


def permute(a, move):
    pairs = []
    for i in range(128):
        y, x, z, k = i // 32, i // 8 % 4, i // 2 % 4, i % 2
        y, x, z, k = (v % 4 for v in move(y, x, z, k))
        pairs.append((i, y * 32 + x * 8 + z * 2 + k))
    return lax.ppermute(a, ("row", "col"), pairs)


def first_axis(a, step):
    return permute(a, lambda y, x, z, k: (y + step * k, x + step * (1 - k), z, k))


def second_axis(a, step):
    return permute(a, lambda y, x, z, k: (y + step * (1 - k), x + step * k, z, k))


def swap_cores(a):
    return permute(a, lambda y, x, z, k: (y, x, z, 1 - k))


def shift(a, axis, step):
    by = [step * (axis == name) for name in "yxz"]
    return permute(a, lambda y, x, z, k: (y + by[0], x + by[1], z + by[2], k))


def plan_tiles(rows, cols, counts, y, x, z, k):
    source = cols // 4
    dy, dx = (source // 4 - y) % 4, (source % 4 - x) % 4
    near, far = jnp.where(k == 0, dx, dy), jnp.where(k == 0, dy, dx)
    triple = (near - (near == 3)) * 4
    slots = cols % 4 + jnp.where(
        far == 0,
        near * 4,
        jnp.where(
            near == 2,
            jnp.where(far == 3, 40, jnp.where(far == 1, 44, 60)),
            triple + jnp.where(far == 1, 16, jnp.where(far == 3, 28, 48)),
        ),
    )
    ids = jnp.arange(256, dtype=jnp.int32)
    owner, ahead = rows // 4 % 2, (rows // 8) ^ z
    away = (ahead == 2) | (ahead == 1 + 2 * owner)
    phase = jnp.where(slots < 16, 0, jnp.where(slots < 40, 1, jnp.where(away, 2, 3)))
    group = phase * 2 + (counts <= 128).astype(jnp.int32)
    key = group * 256 + ids
    rank = jnp.sum((key[None, :] < key[:, None]).astype(jnp.int32), axis=1)
    fields = jnp.stack([ids, rows, slots, counts])
    placed = jnp.sum(jnp.where(rank[None, :, None] == ids[None, None, :], fields[:, :, None], 0), axis=1)
    starts = jnp.sum((group[None, :] < ids[:, None]).astype(jnp.int32), axis=1)
    last = jnp.where(ids < 9, starts, jnp.where(ids == 9, z, k))
    return jnp.concatenate([placed, last[None]], axis=0)


def spmm_kernel(phase, meta, nrow, ncol, value, pieces, *rest):
    rest = list(rest)
    if phase > 0:
        rest.pop(0)
    total = rest.pop(0)
    if phase >= 2:
        keep, give = rest.pop(0), rest.pop(0)
    value32, iota = rest
    value32[...] = value[...].astype(F32)
    iota[...] = lax.broadcasted_iota(jnp.int32, (256, 256), 0).astype(F32).astype(BF)
    if phase == 0:
        total[...] = jnp.zeros_like(total)
    low, middle, high = meta[4, 2 * phase], meta[4, 2 * phase + 1], meta[4, 2 * phase + 2]

    def run(width, begin, steps):
        lane = lax.broadcasted_iota(jnp.int32, (1, width), 1)
        zero = jnp.zeros((256, width), BF)
        one = jnp.ones((256, width), BF)

        def line(ref, tile):
            return ref[pl.ds(tile, 1), :][:, :width]

        def spread(picture, hot):
            index = jnp.broadcast_to(picture.astype(F32).astype(BF), (256, width))
            return jnp.where(iota[:, :width] == index, hot, zero)

        def step(i, carry):
            at = [begin + i * UNROLL + u for u in range(UNROLL)]
            safe = [jnp.minimum(p, high - 1) for p in at]
            tiles = [meta[0, p] for p in safe]
            picked = []
            for u in range(UNROLL):
                piece = pieces[meta[2, safe[u]] - FIRST[phase]]
                columns = spread(line(ncol, tiles[u]), one)
                picked.append(jnp.dot(piece, columns, preferred_element_type=F32).astype(BF))
            for u in range(UNROLL):
                live = jnp.where(at[u] < high, meta[3, safe[u]], 0)
                weight = jnp.where(lane < live, line(value32, tiles[u]), 0.0).astype(BF)
                rows = spread(line(nrow, tiles[u]), jnp.broadcast_to(weight, (256, width)))
                r = meta[1, safe[u]]
                total[r] = total[r] + lax.dot_general(
                    rows, picked[u], (((1,), (1,)), ((), ())), preferred_element_type=F32
                )
            return carry

        lax.fori_loop(0, steps, step, 0)

    wide = (middle - low + UNROLL - 1) // UNROLL
    run(256, low, wide)
    begin = jnp.minimum(low + wide * UNROLL, high)
    run(128, begin, (high - begin + UNROLL - 1) // UNROLL)
    if phase >= 2:
        z, k = meta[4, 9], meta[4, 10]
        near, other = 1 + 2 * k, 3 - 2 * k
        ahead = ((near, other), (2, 2)) if phase == 2 else ((0, 0), (other, near))
        for i, (e_keep, e_give) in enumerate(ahead):
            keep[i] = total[pl.ds(((z ^ e_keep) * 2 + k) * 4, 4)]
            give[i] = total[pl.ds(((z ^ e_give) * 2 + 1 - k) * 4, 4)].astype(BF)


def spmm(phase, meta, nrow, ncol, value, pieces, total=None):
    vmem = pl.BlockSpec(memory_space=pltpu.VMEM)
    args = [nrow, ncol, value, pieces] + ([] if total is None else [total])
    out = [jax.ShapeDtypeStruct((32, 256, 128), F32)]
    if phase >= 2:
        out += [jax.ShapeDtypeStruct((2, 4, 256, 128), F32), jax.ShapeDtypeStruct((2, 4, 256, 128), BF)]
    share = (16, 24, 12, 12)[phase] / 64
    return pl.pallas_call(
        functools.partial(spmm_kernel, phase),
        out_shape=out,
        in_specs=[pl.BlockSpec(memory_space=pltpu.SMEM)] + [vmem] * len(args),
        out_specs=[vmem] * len(out),
        scratch_shapes=[pltpu.VMEM((256, 256), F32), pltpu.VMEM((256, 256), BF)],
        input_output_aliases={} if total is None else {5: 0},
        compiler_params=pltpu.CompilerParams(vmem_limit_bytes=40 << 20),
        cost_estimate=pl.CostEstimate(flops=int(share * 2.0e10), bytes_accessed=1 << 20, transcendentals=0),
        name=f"spmm_phase{phase}",
    )(meta, *args)


def finish_kernel(hidden, weight, cotangent, node_out, partial):
    w = weight[...].astype(F32)
    grad = jnp.zeros((128, 128), F32)
    for i in range(4):
        h = hidden[i]
        pre = jnp.dot(h, w, precision=lax.Precision.HIGHEST, preferred_element_type=F32)
        sig = 1.0 / (1.0 + jnp.exp(-pre))
        span = pl.ds(i * 256, 256)
        node_out[span, :] = (pre * sig).astype(BF)
        slope = sig * (1.0 + pre * (1.0 - sig))
        pre_grad = (cotangent[span, :].astype(F32) * slope).astype(BF).astype(F32)
        grad = grad + lax.dot_general(
            h, pre_grad, (((0,), (0,)), ((), ())), precision=lax.Precision.HIGHEST, preferred_element_type=F32
        )
    partial[...] = grad


def finish(hidden, weight, cotangent):
    vmem = pl.BlockSpec(memory_space=pltpu.VMEM)
    return pl.pallas_call(
        finish_kernel,
        out_shape=[jax.ShapeDtypeStruct((1024, 128), BF), jax.ShapeDtypeStruct((128, 128), F32)],
        in_specs=[vmem] * 3,
        out_specs=[vmem] * 2,
        compiler_params=pltpu.CompilerParams(vmem_limit_bytes=16 << 20),
        name="finish",
    )(hidden, weight, cotangent)


def transpose_kernel(features, out):
    for i in range(4):
        out[i] = features[pl.ds(i * 256, 256), :].T


def transposed(features):
    vmem = pl.BlockSpec(memory_space=pltpu.VMEM)
    return pl.pallas_call(
        transpose_kernel,
        out_shape=jax.ShapeDtypeStruct((4, 128, 256), BF),
        in_specs=[vmem],
        out_specs=vmem,
        compiler_params=pltpu.CompilerParams(vmem_limit_bytes=8 << 20),
        name="transposed",
    )(features)


def cat(*parts):
    return jnp.concatenate(parts, axis=0)


def add(a, b):
    return a.astype(F32) + b.astype(F32)


def sum_ring(v, axis):
    sent = v.astype(BF)
    beside = permute(sent, lambda y, x, z, k: tuple(
        c + (1 - 2 * k) * (axis == name) for c, name in ((y, "y"), (x, "x"), (z, "z"))) + (k,))
    across = shift(sent, axis, 2).astype(F32)
    return (lax.reduce_precision(v, 8, 7) + across) + add(beside, swap_cores(beside))


def body(features, weight, cotangent, tile_row, tile_col, nnz_row, nnz_col, edge_value, tile_count):
    row, col = lax.axis_index("row"), lax.axis_index("col")
    meta = plan_tiles(
        tile_row.reshape(256), tile_col.reshape(256), tile_count.reshape(256),
        row // 4, row % 4, col // 2, col % 2,
    )
    slots = (meta, nnz_row.reshape(256, 256), nnz_col.reshape(256, 256), edge_value.reshape(256, 256))

    own = transposed(features)
    right, left = first_axis(own, 1), first_axis(own, -1)
    opposite = first_axis(own, 2)
    near = cat(own, left, right)
    down, up = second_axis(near, 1), second_axis(near, -1)
    corner = second_axis(opposite, 2)
    (total,) = spmm(0, *slots, cat(own, left, opposite, right))
    plus = second_axis(cat(opposite, down[:PLUS]), 1)
    minus = second_axis(cat(opposite, up[PLUS:]), -1)
    (total,) = spmm(1, *slots, cat(up, down), total)
    rest = cat(plus[:4], minus[:4], plus[4:], minus[4:], corner)
    total, keep, give = spmm(2, *slots, rest, total)

    away = add(keep, swap_cores(give)).astype(BF)
    away, total = lax.optimization_barrier((away, total))
    got = permute(away, lambda y, x, z, k: (y, x, z ^ (1 + 2 * k), k))
    total, keep, give = spmm(3, *slots, rest, total)
    give, got = lax.optimization_barrier((give, got))
    home = add(keep, swap_cores(give))
    mine, pair = add(home[0], got[0]), add(home[1], got[1])
    hidden = add(mine, permute(pair.astype(BF), lambda y, x, z, k: (y, x, z ^ (3 - 2 * k), k)))

    node_out, grad = finish(hidden, weight, cotangent)
    grad = grad + swap_cores(grad)
    for axis in ("z", "x", "y"):
        grad = sum_ring(grad, axis)
    return node_out, grad


def solution(mesh):
    placed = (
        P(("col", "row"), None),
        P(),
        P(("row", "col"), None),
        P("row", "col", None),
        P("row", "col", None),
        P("row", "col", None, None),
        P("row", "col", None, None),
        P("row", "col", None, None),
        P("row", "col", None),
    )
    return jax.shard_map(
        body, mesh=mesh, in_specs=placed, out_specs=(P(("row", "col"), None), P()), check_vma=False
    )
```

```python
import functools

import jax
import jax.numpy as jnp
from jax import lax
from jax.experimental import pallas as pl
from jax.experimental.pallas import tpu as pltpu
from jax.sharding import PartitionSpec as P

BF = jnp.bfloat16
F32 = jnp.float32
UNROLL = 16
FIRST = (0, 16, 40, 40)
PLUS = 6


def permute(a, move):
    pairs = []
    for i in range(128):
        y, x, z, k = i // 32, i // 8 % 4, i // 2 % 4, i % 2
        y, x, z, k = (v % 4 for v in move(y, x, z, k))
        pairs.append((i, y * 32 + x * 8 + z * 2 + k))
    return lax.ppermute(a, ("row", "col"), pairs)


def first_axis(a, step):
    return permute(a, lambda y, x, z, k: (y + step * k, x + step * (1 - k), z, k))


def second_axis(a, step):
    return permute(a, lambda y, x, z, k: (y + step * (1 - k), x + step * k, z, k))


def swap_cores(a):
    return permute(a, lambda y, x, z, k: (y, x, z, 1 - k))


def shift(a, axis, step):
    by = [step * (axis == name) for name in "yxz"]
    return permute(a, lambda y, x, z, k: (y + by[0], x + by[1], z + by[2], k))


def plan_tiles(rows, cols, counts, y, x, z, k):
    source = cols // 4
    dy, dx = (source // 4 - y) % 4, (source % 4 - x) % 4
    near, far = jnp.where(k == 0, dx, dy), jnp.where(k == 0, dy, dx)
    triple = (near - (near == 3)) * 4
    slots = cols % 4 + jnp.where(
        far == 0,
        near * 4,
        jnp.where(
            near == 2,
            jnp.where(far == 3, 40, jnp.where(far == 1, 44, 60)),
            triple + jnp.where(far == 1, 16, jnp.where(far == 3, 28, 48)),
        ),
    )
    ids = jnp.arange(256, dtype=jnp.int32)
    owner, ahead = rows // 4 % 2, (rows // 8) ^ z
    away = (ahead == 2) | (ahead == 1 + 2 * owner)
    phase = jnp.where(slots < 16, 0, jnp.where(slots < 40, 1, jnp.where(away, 2, 3)))
    group = phase * 2 + (counts <= 128).astype(jnp.int32)
    key = group * 256 + ids
    rank = jnp.sum((key[None, :] < key[:, None]).astype(jnp.int32), axis=1)
    fields = jnp.stack([ids, rows, slots, counts])
    placed = jnp.sum(jnp.where(rank[None, :, None] == ids[None, None, :], fields[:, :, None], 0), axis=1)
    starts = jnp.sum((group[None, :] < ids[:, None]).astype(jnp.int32), axis=1)
    last = jnp.where(ids < 9, starts, jnp.where(ids == 9, z, k))
    return jnp.concatenate([placed, last[None]], axis=0)


def spmm_kernel(phase, meta, nrow, ncol, value, pieces, *rest):
    rest = list(rest)
    if phase > 0:
        rest.pop(0)
    total = rest.pop(0)
    if phase >= 2:
        keep, give = rest.pop(0), rest.pop(0)
    value32, iota = rest
    value32[...] = value[...].astype(F32)
    iota[...] = lax.broadcasted_iota(jnp.int32, (256, 256), 0).astype(F32).astype(BF)
    if phase == 0:
        total[...] = jnp.zeros_like(total)
    low, middle, high = meta[4, 2 * phase], meta[4, 2 * phase + 1], meta[4, 2 * phase + 2]

    def run(width, begin, steps):
        lane = lax.broadcasted_iota(jnp.int32, (1, width), 1)
        zero = jnp.zeros((256, width), BF)
        one = jnp.ones((256, width), BF)

        def line(ref, tile):
            return ref[pl.ds(tile, 1), :][:, :width]

        def spread(picture, hot):
            index = jnp.broadcast_to(picture.astype(F32).astype(BF), (256, width))
            return jnp.where(iota[:, :width] == index, hot, zero)

        def step(i, carry):
            at = [begin + i * UNROLL + u for u in range(UNROLL)]
            safe = [jnp.minimum(p, high - 1) for p in at]
            tiles = [meta[0, p] for p in safe]
            picked = []
            for u in range(UNROLL):
                piece = pieces[meta[2, safe[u]] - FIRST[phase]]
                columns = spread(line(ncol, tiles[u]), one)
                picked.append(jnp.dot(piece, columns, preferred_element_type=F32).astype(BF))
            for u in range(UNROLL):
                live = jnp.where(at[u] < high, meta[3, safe[u]], 0)
                weight = jnp.where(lane < live, line(value32, tiles[u]), 0.0).astype(BF)
                rows = spread(line(nrow, tiles[u]), jnp.broadcast_to(weight, (256, width)))
                r = meta[1, safe[u]]
                total[r] = total[r] + lax.dot_general(
                    rows, picked[u], (((1,), (1,)), ((), ())), preferred_element_type=F32
                )
            return carry

        lax.fori_loop(0, steps, step, 0)

    wide = (middle - low + UNROLL - 1) // UNROLL
    run(256, low, wide)
    begin = jnp.minimum(low + wide * UNROLL, high)
    run(128, begin, (high - begin + UNROLL - 1) // UNROLL)
    if phase >= 2:
        z, k = meta[4, 9], meta[4, 10]
        near, other = 1 + 2 * k, 3 - 2 * k
        ahead = ((near, other), (2, 2)) if phase == 2 else ((0, 0), (other, near))
        for i, (e_keep, e_give) in enumerate(ahead):
            keep[i] = total[pl.ds(((z ^ e_keep) * 2 + k) * 4, 4)]
            give[i] = total[pl.ds(((z ^ e_give) * 2 + 1 - k) * 4, 4)].astype(BF)


def spmm(phase, meta, nrow, ncol, value, pieces, total=None):
    vmem = pl.BlockSpec(memory_space=pltpu.VMEM)
    args = [nrow, ncol, value, pieces] + ([] if total is None else [total])
    out = [jax.ShapeDtypeStruct((32, 256, 128), F32)]
    if phase >= 2:
        out += [jax.ShapeDtypeStruct((2, 4, 256, 128), F32), jax.ShapeDtypeStruct((2, 4, 256, 128), BF)]
    share = (16, 24, 12, 12)[phase] / 64
    return pl.pallas_call(
        functools.partial(spmm_kernel, phase),
        out_shape=out,
        in_specs=[pl.BlockSpec(memory_space=pltpu.SMEM)] + [vmem] * len(args),
        out_specs=[vmem] * len(out),
        scratch_shapes=[pltpu.VMEM((256, 256), F32), pltpu.VMEM((256, 256), BF)],
        input_output_aliases={} if total is None else {5: 0},
        compiler_params=pltpu.CompilerParams(vmem_limit_bytes=40 << 20),
        cost_estimate=pl.CostEstimate(flops=int(share * 2.0e10), bytes_accessed=1 << 20, transcendentals=0),
        name=f"spmm_phase{phase}",
    )(meta, *args)


def finish_kernel(hidden, weight, cotangent, node_out, partial):
    w = weight[...].astype(F32)
    grad = jnp.zeros((128, 128), F32)
    for i in range(4):
        h = hidden[i]
        pre = jnp.dot(h, w, precision=lax.Precision.HIGHEST, preferred_element_type=F32)
        sig = 1.0 / (1.0 + jnp.exp(-pre))
        span = pl.ds(i * 256, 256)
        node_out[span, :] = (pre * sig).astype(BF)
        slope = sig * (1.0 + pre * (1.0 - sig))
        pre_grad = (cotangent[span, :].astype(F32) * slope).astype(BF).astype(F32)
        grad = grad + lax.dot_general(
            h, pre_grad, (((0,), (0,)), ((), ())), precision=lax.Precision.HIGHEST, preferred_element_type=F32
        )
    partial[...] = grad


def finish(hidden, weight, cotangent):
    vmem = pl.BlockSpec(memory_space=pltpu.VMEM)
    return pl.pallas_call(
        finish_kernel,
        out_shape=[jax.ShapeDtypeStruct((1024, 128), BF), jax.ShapeDtypeStruct((128, 128), F32)],
        in_specs=[vmem] * 3,
        out_specs=[vmem] * 2,
        compiler_params=pltpu.CompilerParams(vmem_limit_bytes=16 << 20),
        name="finish",
    )(hidden, weight, cotangent)


def transpose_kernel(features, out):
    for i in range(4):
        out[i] = features[pl.ds(i * 256, 256), :].T


def transposed(features):
    vmem = pl.BlockSpec(memory_space=pltpu.VMEM)
    return pl.pallas_call(
        transpose_kernel,
        out_shape=jax.ShapeDtypeStruct((4, 128, 256), BF),
        in_specs=[vmem],
        out_specs=vmem,
        compiler_params=pltpu.CompilerParams(vmem_limit_bytes=8 << 20),
        name="transposed",
    )(features)


def cat(*parts):
    return jnp.concatenate(parts, axis=0)


def add(a, b):
    return a.astype(F32) + b.astype(F32)


def sum_ring(v, axis):
    sent = v.astype(BF)
    beside = permute(sent, lambda y, x, z, k: tuple(
        c + (1 - 2 * k) * (axis == name) for c, name in ((y, "y"), (x, "x"), (z, "z"))) + (k,))
    across = shift(sent, axis, 2).astype(F32)
    return (lax.reduce_precision(v, 8, 7) + across) + add(beside, swap_cores(beside))


def body(features, weight, cotangent, tile_row, tile_col, nnz_row, nnz_col, edge_value, tile_count):
    row, col = lax.axis_index("row"), lax.axis_index("col")
    meta = plan_tiles(
        tile_row.reshape(256), tile_col.reshape(256), tile_count.reshape(256),
        row // 4, row % 4, col // 2, col % 2,
    )
    slots = (meta, nnz_row.reshape(256, 256), nnz_col.reshape(256, 256), edge_value.reshape(256, 256))

    own = transposed(features)
    right, left = first_axis(own, 1), first_axis(own, -1)
    opposite = first_axis(own, 2)
    near = cat(own, left, right)
    down, up = second_axis(near, 1), second_axis(near, -1)
    corner = second_axis(opposite, 2)
    (total,) = spmm(0, *slots, cat(own, left, opposite, right))
    plus = second_axis(cat(opposite, down[:PLUS]), 1)
    minus = second_axis(cat(opposite, up[PLUS:]), -1)
    (total,) = spmm(1, *slots, cat(up, down), total)
    rest = cat(plus[:4], minus[:4], plus[4:], minus[4:], corner)
    total, keep, give = spmm(2, *slots, rest, total)

    away = add(keep, swap_cores(give)).astype(BF)
    away, total = lax.optimization_barrier((away, total))

    def first_chip(a):
        return permute(a, lambda y, x, z, k: (y, x, z ^ (1 + 2 * k), k))

    got_far, got_near = first_chip(away[1]), first_chip(away[0])
    total, keep, give = spmm(3, *slots, rest, total)
    give, got_far = lax.optimization_barrier((give, got_far))
    home = add(keep, swap_cores(give))
    pair = add(home[1], got_far).astype(BF)
    hidden = add(add(home[0], got_near), permute(pair, lambda y, x, z, k: (y, x, z ^ (3 - 2 * k), k)))

    node_out, grad = finish(hidden, weight, cotangent)
    grad = grad + swap_cores(grad)
    for axis in ("z", "x", "y"):
        grad = sum_ring(grad, axis)
    return node_out, grad


def solution(mesh):
    placed = (
        P(("col", "row"), None),
        P(),
        P(("row", "col"), None),
        P("row", "col", None),
        P("row", "col", None),
        P("row", "col", None, None),
        P("row", "col", None, None),
        P("row", "col", None, None),
        P("row", "col", None),
    )
    return jax.shard_map(
        body, mesh=mesh, in_specs=placed, out_specs=(P(("row", "col"), None), P()), check_vma=False
    )
```

```python
import functools

import jax
import jax.numpy as jnp
from jax import lax
from jax.experimental import pallas as pl
from jax.experimental.pallas import tpu as pltpu
from jax.sharding import PartitionSpec as P

BF = jnp.bfloat16
F32 = jnp.float32
UNROLL = 16
FIRST = (0, 16, 40, 40)
PLUS = 6


def permute(a, move):
    pairs = []
    for i in range(128):
        y, x, z, k = i // 32, i // 8 % 4, i // 2 % 4, i % 2
        y, x, z, k = (v % 4 for v in move(y, x, z, k))
        pairs.append((i, y * 32 + x * 8 + z * 2 + k))
    return lax.ppermute(a, ("row", "col"), pairs)


def first_axis(a, step):
    return permute(a, lambda y, x, z, k: (y + step * k, x + step * (1 - k), z, k))


def second_axis(a, step):
    return permute(a, lambda y, x, z, k: (y + step * (1 - k), x + step * k, z, k))


def swap_cores(a):
    return permute(a, lambda y, x, z, k: (y, x, z, 1 - k))


def shift(a, axis, step):
    by = [step * (axis == name) for name in "yxz"]
    return permute(a, lambda y, x, z, k: (y + by[0], x + by[1], z + by[2], k))


def plan_tiles(rows, cols, counts, y, x, z, k):
    source = cols // 4
    dy, dx = (source // 4 - y) % 4, (source % 4 - x) % 4
    near, far = jnp.where(k == 0, dx, dy), jnp.where(k == 0, dy, dx)
    triple = (near - (near == 3)) * 4
    slots = cols % 4 + jnp.where(
        far == 0,
        near * 4,
        jnp.where(
            near == 2,
            jnp.where(far == 3, 40, jnp.where(far == 1, 44, 60)),
            triple + jnp.where(far == 1, 16, jnp.where(far == 3, 28, 48)),
        ),
    )
    ids = jnp.arange(256, dtype=jnp.int32)
    owner, ahead = rows // 4 % 2, (rows // 8) ^ z
    away = (ahead == 2) | (ahead == 1 + 2 * owner)
    phase = jnp.where(slots < 16, 0, jnp.where(slots < 40, 1, jnp.where(away, 2, 3)))
    group = phase * 2 + (counts <= 128).astype(jnp.int32)
    key = group * 256 + ids
    rank = jnp.sum((key[None, :] < key[:, None]).astype(jnp.int32), axis=1)
    fields = jnp.stack([ids, rows, slots, counts])
    placed = jnp.sum(jnp.where(rank[None, :, None] == ids[None, None, :], fields[:, :, None], 0), axis=1)
    starts = jnp.sum((group[None, :] < ids[:, None]).astype(jnp.int32), axis=1)
    last = jnp.where(ids < 9, starts, jnp.where(ids == 9, z, k))
    return jnp.concatenate([placed, last[None]], axis=0)


def spmm_kernel(phase, meta, nrow, ncol, value, pieces, *rest):
    rest = list(rest)
    if phase > 0:
        rest.pop(0)
    total = rest.pop(0)
    if phase >= 2:
        keep, give = rest.pop(0), rest.pop(0)
    value32, iota = rest
    value32[...] = value[...].astype(F32)
    iota[...] = lax.broadcasted_iota(jnp.int32, (256, 256), 0).astype(F32).astype(BF)
    if phase == 0:
        total[...] = jnp.zeros_like(total)
    low, middle, high = meta[4, 2 * phase], meta[4, 2 * phase + 1], meta[4, 2 * phase + 2]

    def run(width, begin, steps):
        lane = lax.broadcasted_iota(jnp.int32, (1, width), 1)
        zero = jnp.zeros((256, width), BF)
        one = jnp.ones((256, width), BF)

        def line(ref, tile):
            return ref[pl.ds(tile, 1), :][:, :width]

        def spread(picture, hot):
            index = jnp.broadcast_to(picture.astype(F32).astype(BF), (256, width))
            return jnp.where(iota[:, :width] == index, hot, zero)

        def step(i, carry):
            at = [begin + i * UNROLL + u for u in range(UNROLL)]
            safe = [jnp.minimum(p, high - 1) for p in at]
            tiles = [meta[0, p] for p in safe]
            picked = []
            for u in range(UNROLL):
                piece = pieces[meta[2, safe[u]] - FIRST[phase]]
                columns = spread(line(ncol, tiles[u]), one)
                picked.append(jnp.dot(piece, columns, preferred_element_type=F32).astype(BF))
            for u in range(UNROLL):
                live = jnp.where(at[u] < high, meta[3, safe[u]], 0)
                weight = jnp.where(lane < live, line(value32, tiles[u]), 0.0).astype(BF)
                rows = spread(line(nrow, tiles[u]), jnp.broadcast_to(weight, (256, width)))
                r = meta[1, safe[u]]
                total[r] = total[r] + lax.dot_general(
                    rows, picked[u], (((1,), (1,)), ((), ())), preferred_element_type=F32
                )
            return carry

        lax.fori_loop(0, steps, step, 0)

    wide = (middle - low + UNROLL - 1) // UNROLL
    run(256, low, wide)
    begin = jnp.minimum(low + wide * UNROLL, high)
    run(128, begin, (high - begin + UNROLL - 1) // UNROLL)
    if phase >= 2:
        z, k = meta[4, 9], meta[4, 10]
        near, other = 1 + 2 * k, 3 - 2 * k
        ahead = ((near, other), (2, 2)) if phase == 2 else ((0, 0), (other, near))
        for i, (e_keep, e_give) in enumerate(ahead):
            keep[i] = total[pl.ds(((z ^ e_keep) * 2 + k) * 4, 4)]
            give[i] = total[pl.ds(((z ^ e_give) * 2 + 1 - k) * 4, 4)].astype(BF)


def spmm(phase, meta, nrow, ncol, value, pieces, total=None):
    vmem = pl.BlockSpec(memory_space=pltpu.VMEM)
    args = [nrow, ncol, value, pieces] + ([] if total is None else [total])
    out = [jax.ShapeDtypeStruct((32, 256, 128), F32)]
    if phase >= 2:
        out += [jax.ShapeDtypeStruct((2, 4, 256, 128), F32), jax.ShapeDtypeStruct((2, 4, 256, 128), BF)]
    share = (16, 24, 12, 12)[phase] / 64
    return pl.pallas_call(
        functools.partial(spmm_kernel, phase),
        out_shape=out,
        in_specs=[pl.BlockSpec(memory_space=pltpu.SMEM)] + [vmem] * len(args),
        out_specs=[vmem] * len(out),
        scratch_shapes=[pltpu.VMEM((256, 256), F32), pltpu.VMEM((256, 256), BF)],
        input_output_aliases={} if total is None else {5: 0},
        compiler_params=pltpu.CompilerParams(vmem_limit_bytes=40 << 20),
        cost_estimate=pl.CostEstimate(flops=int(share * 2.0e10), bytes_accessed=1 << 20, transcendentals=0),
        name=f"spmm_phase{phase}",
    )(meta, *args)


def two_parts(v):
    high = v.astype(BF)
    return high, (v - high.astype(F32)).astype(BF)


def finish_kernel(hidden, weight, cotangent, node_out, partial):
    w = weight[...]
    grad = jnp.zeros((128, 128), F32)
    for i in range(4):
        parts = two_parts(hidden[i])
        pre = sum(jnp.dot(part, w, preferred_element_type=F32) for part in parts)
        sig = 1.0 / (1.0 + jnp.exp(-pre))
        span = pl.ds(i * 256, 256)
        node_out[span, :] = (pre * sig).astype(BF)
        slope = sig * (1.0 + pre * (1.0 - sig))
        pre_grad = (cotangent[span, :].astype(F32) * slope).astype(BF)
        for part in parts:
            grad = grad + lax.dot_general(part, pre_grad, (((0,), (0,)), ((), ())), preferred_element_type=F32)
    partial[...] = grad


def finish(hidden, weight, cotangent):
    vmem = pl.BlockSpec(memory_space=pltpu.VMEM)
    return pl.pallas_call(
        finish_kernel,
        out_shape=[jax.ShapeDtypeStruct((1024, 128), BF), jax.ShapeDtypeStruct((128, 128), F32)],
        in_specs=[vmem] * 3,
        out_specs=[vmem] * 2,
        compiler_params=pltpu.CompilerParams(vmem_limit_bytes=16 << 20),
        name="finish",
    )(hidden, weight, cotangent)


def transpose_kernel(features, out):
    for i in range(4):
        out[i] = features[pl.ds(i * 256, 256), :].T


def transposed(features):
    vmem = pl.BlockSpec(memory_space=pltpu.VMEM)
    return pl.pallas_call(
        transpose_kernel,
        out_shape=jax.ShapeDtypeStruct((4, 128, 256), BF),
        in_specs=[vmem],
        out_specs=vmem,
        compiler_params=pltpu.CompilerParams(vmem_limit_bytes=8 << 20),
        name="transposed",
    )(features)


def cat(*parts):
    return jnp.concatenate(parts, axis=0)


def add(a, b):
    return a.astype(F32) + b.astype(F32)


def sum_ring(v, axis):
    sent = v.astype(BF)
    beside = permute(sent, lambda y, x, z, k: tuple(
        c + (1 - 2 * k) * (axis == name) for c, name in ((y, "y"), (x, "x"), (z, "z"))) + (k,))
    across = shift(sent, axis, 2).astype(F32)
    return (lax.reduce_precision(v, 8, 7) + across) + add(beside, swap_cores(beside))


def body(features, weight, cotangent, tile_row, tile_col, nnz_row, nnz_col, edge_value, tile_count):
    row, col = lax.axis_index("row"), lax.axis_index("col")
    meta = plan_tiles(
        tile_row.reshape(256), tile_col.reshape(256), tile_count.reshape(256),
        row // 4, row % 4, col // 2, col % 2,
    )
    slots = (meta, nnz_row.reshape(256, 256), nnz_col.reshape(256, 256), edge_value.reshape(256, 256))

    own = transposed(features)
    right, left = first_axis(own, 1), first_axis(own, -1)
    opposite = first_axis(own, 2)
    near = cat(own, left, right)
    down, up = second_axis(near, 1), second_axis(near, -1)
    corner = second_axis(opposite, 2)
    (total,) = spmm(0, *slots, cat(own, left, opposite, right))
    plus = second_axis(cat(opposite, down[:PLUS]), 1)
    minus = second_axis(cat(opposite, up[PLUS:]), -1)
    (total,) = spmm(1, *slots, cat(up, down), total)
    rest = cat(plus[:4], minus[:4], plus[4:], minus[4:], corner)
    total, keep, give = spmm(2, *slots, rest, total)

    away = add(keep, swap_cores(give)).astype(BF)
    away, total = lax.optimization_barrier((away, total))

    def first_chip(a):
        return permute(a, lambda y, x, z, k: (y, x, z ^ (1 + 2 * k), k))

    got_far, got_near = first_chip(away[1]), first_chip(away[0])
    total, keep, give = spmm(3, *slots, rest, total)
    give, got_far = lax.optimization_barrier((give, got_far))
    home = add(keep, swap_cores(give))
    pair = add(home[1], got_far).astype(BF)
    hidden = add(add(home[0], got_near), permute(pair, lambda y, x, z, k: (y, x, z ^ (3 - 2 * k), k)))

    node_out, grad = finish(hidden, weight, cotangent)
    grad = grad + swap_cores(grad)
    for axis in ("z", "x", "y"):
        grad = sum_ring(grad, axis)
    return node_out, grad


def solution(mesh):
    placed = (
        P(("col", "row"), None),
        P(),
        P(("row", "col"), None),
        P("row", "col", None),
        P("row", "col", None),
        P("row", "col", None, None),
        P("row", "col", None, None),
        P("row", "col", None, None),
        P("row", "col", None),
    )
    return jax.shard_map(
        body, mesh=mesh, in_specs=placed, out_specs=(P(("row", "col"), None), P()), check_vma=False
    )
```
